32 devices in a mesh: band: 2 (over x), row: 16 (over z, y, core).
Axes of the slice: x: 2, y: 2, z: 4, core: 2. Of those that a mesh axis runs over, the one named last changes fastest.
Arguments:
- tiles: bfloat16 [256, 96, 64, 128], P(('band', 'row')), parts along dimension 0, may hold values from -0.0390625 to 0.0390625
- tile_light: int32 [256, 96], P(('band', 'row')), parts along dimension 0, may hold values from 0 to 255
- tile_count: int32 [256], P(('band', 'row')), parts along dimension 0, may hold values from 24 to 96, as said below
- env_maps: bfloat16 [16384, 384], P('row'), may hold values from 0.099609375 to 10
- frame_slot: int32 [128], replicated, may hold values from 0 to 127, each once
Outputs:
- frames: bfloat16 [128, 32768], P('row', 'band'), parts along dimension 1
The draws below stay inside these ranges and needn't reach their ends.
There are 2 independent parts, one for each index of `band`. The reference program is written for one: setup_inputs(seed, part) draws one part's arguments, and reference() takes and returns one part's arrays. A program takes and returns all parts, laid end to end along the dimension named above; an argument that names none is the same for every part. Nothing has to cross between parts.
Inputs may be any that keep to these rules, and one draw needn't show every extreme that they name: `tile_count`: every block has at least a quarter of the slots used, and some block uses all 96.
All inputs are finite; a program needn't handle non-finite values.
Results may differ from the reference program's by a relative error of at most 0.001.
Values may be sent and summed in bfloat16 or wider, within the bound.
A program may use at most 128 MiB of HBM per device.

```python
import math
import jax
import jax.numpy as jnp
from jax import lax

LIGHTS = 16384
F = 128
CHANNELS = 3
TMAX = 96
RB_DEV = 8
ROWBLK = 128


def draw_tile_count(key, part):
    key = jax.random.fold_in(key, 11)
    key_counts, key_place = jax.random.split(key)
    counts = jax.random.randint(key_counts, (ROWBLK,), max(1, TMAX // 4), TMAX + 1)
    position = jax.random.randint(key_place, (), 0, ROWBLK)
    return counts.at[position].set(TMAX).astype(jnp.int32)


def place_ends(array, rng, low, high):
    longest = array.shape.index(max(array.shape))
    spots = []
    for shift in (0, 1):
        where = [jax.random.randint(jax.random.fold_in(rng, axis), (), 0, length) for axis, length in enumerate(array.shape)]
        where[longest] = (where[longest] + shift) % array.shape[longest]
        spots.append(tuple(where))
    return array.at[spots[0]].set(low).at[spots[1]].set(high)


def level_of(key, extent, cuts, least, largest):
    def one(axis_at, blocks):
        draws = jax.random.uniform(jax.random.fold_in(jax.random.fold_in(key, 6), axis_at), (blocks,), jnp.float32, least / len(cuts), largest / len(cuts))
        return jnp.repeat(jnp.exp(draws), extent[axis_at] // blocks).reshape((-1,) + (1,) * (len(extent) - axis_at - 1))

    level = one(*cuts[0])
    for cut in cuts[1:]:
        level = level * one(*cut)
    return level


def noise(stream_key, dims, scale, most, pieces=(), held_as=jnp.bfloat16):
    drawn = scale * jax.random.normal(stream_key, dims, jnp.float32)
    if pieces:
        drawn = drawn * level_of(stream_key, dims, pieces, -0.22, 0.18)
    return jnp.clip(drawn, -most, most).astype(held_as)


def setup_inputs(seed: int = 0, part: int = 0) -> dict:
    keys = jax.random.split(jax.random.key(seed), 6)
    part_keys = jax.random.split(jax.random.fold_in(keys[5], part), 6)
    tiles = noise(part_keys[0], (ROWBLK, TMAX, 64, 128), (TMAX * 256) ** -0.5, 0.0390625, ((0, 16),))
    tile_light = place_ends(jax.random.randint(part_keys[1], (ROWBLK, TMAX), 0, LIGHTS // 64), jax.random.fold_in(part_keys[1], 1), 0, (LIGHTS // 64) - 1).astype(jnp.int32)
    tile_count = draw_tile_count(jax.random.fold_in(jax.random.fold_in(keys[5], part), 71), part)
    env_maps = jnp.clip(jnp.exp(math.log(10.0) - 4.609084 * jax.random.uniform(keys[3], (LIGHTS, CHANNELS * F), jnp.float32) ** level_of(keys[3], (LIGHTS, CHANNELS * F), ((0, 16),), -0.2, 0.2)), 0.099609375, 10.0).astype(jnp.bfloat16)
    frame_slot = jax.random.permutation(keys[4], F).astype(jnp.int32)
    return dict(tiles=tiles, tile_light=tile_light, tile_count=tile_count, env_maps=env_maps, frame_slot=frame_slot)


def reference(tiles, tile_light, tile_count, env_maps, frame_slot):
    blocks = env_maps.reshape(LIGHTS // 64, 64, CHANNELS, F)

    def relight_block(packed):
        index, tile_rows, lights, tile_total = packed
        channel = (index // RB_DEV) % CHANNELS
        chosen = lax.dynamic_index_in_dim(blocks, channel, 2, keepdims=False)[lights]
        active = (jnp.arange(TMAX, dtype=jnp.int32) < tile_total).astype(jnp.float32)
        product = jnp.einsum("slr,slf,s->fr", tile_rows.astype(jnp.float32), chosen.astype(jnp.float32), active)
        return product.astype(jnp.bfloat16)

    relit_image = lax.map(relight_block, (jnp.arange(ROWBLK, dtype=jnp.int32), tiles, tile_light, tile_count))
    relit_image = relit_image[:, frame_slot, :]
    return relit_image.transpose(1, 0, 2).reshape(F, ROWBLK * 128)
```

```python
import functools
import jax
import jax.numpy as jnp
from jax import lax
from jax.experimental import pallas as pl
from jax.experimental.pallas import tpu as pltpu
from jax.sharding import PartitionSpec as P

F = 128
CHANNELS = 3
DEPTH = 64
J = 4
JC = 2
MESH = pl.DeviceIdType.MESH


def kernel(Z, W, light, count, slot, env, tiles, out,
           own, trunk, emap, dup, tv, sb, zs, zr, fs, fr, xs, xr, ts, os_, or_):
    R = 4 * Z
    G, slots = light.shape
    L = env.shape[0]
    KJ = F // J
    KC = F // JC
    fpd = F // R
    X = L - W
    x = lax.axis_index("band")
    row = lax.axis_index("row")
    core = lax.rem(row, 2)
    y = lax.rem(lax.div(row, 2), 2)
    z = lax.div(row, 4)
    me4 = y * 2 + core
    mych = lax.rem(row, CHANNELS)
    off = pl.multiple_of(x * X, 128)
    xoff = pl.multiple_of(x * W, 128)
    xland = pl.multiple_of((1 - x) * W, 128)

    barrier = pltpu.get_barrier_semaphore()

    def greet(i, _):
        pl.semaphore_signal(barrier, inc=1, device_id=(x, lax.rem(row + i, R)), device_id_type=MESH)
        return 0

    lax.fori_loop(1, R, greet, 0)
    pl.semaphore_signal(barrier, inc=1, device_id=(1 - x, row), device_id_type=MESH)

    def tile_copy(g):
        return pltpu.make_async_copy(tiles.at[g], tv.at[g], ts.at[g])

    perm = (slot[...] == lax.broadcasted_iota(jnp.int32, (F, F), 1)).astype(jnp.float32).astype(jnp.bfloat16)
    for c in range(CHANNELS):
        own[c] = lax.dot_general(perm, env[:, c * F:(c + 1) * F], (((1,), (1,)), ((), ())),
                                 preferred_element_type=jnp.float32).astype(jnp.bfloat16)
    for jc in range(JC):
        dup[jc, dup.shape[1] - 1] = jnp.zeros((KC, 128), jnp.bfloat16)

    pl.semaphore_wait(barrier, R)

    def rows_of(j):
        return pl.ds(pl.multiple_of(j * KJ, KJ), KJ)

    def z_copy(j, zz, up, mine):
        rows = rows_of(j)
        src = own.at[:, rows, pl.ds(off, W)] if mine else trunk.at[zz, :, rows, :]
        to = row + 4 if up else row - 4
        return pltpu.make_async_remote_copy(
            src_ref=src, dst_ref=trunk.at[zz, :, rows, :],
            send_sem=zs.at[j, 0 if up else 1, zz], recv_sem=zr.at[j, zz],
            device_id=(x, to), device_id_type=MESH)

    def z_wait(j, zz):
        here = trunk.at[zz, :, rows_of(j), :]
        pltpu.make_async_remote_copy(
            src_ref=here, dst_ref=here, send_sem=zs.at[j, 0, zz], recv_sem=zr.at[j, zz],
            device_id=(x, row), device_id_type=MESH).wait_recv()

    def peer(k):
        y2 = 1 - y if k // 2 else y
        c2 = 1 - core if k % 2 else core
        return y2, c2

    def fan_copy(j, zz, k, mine):
        y2, c2 = peer(k)
        to = (z * 2 + y2) * 2 + c2
        ch = lax.rem(to, CHANNELS)
        rows = rows_of(j)
        if mine:
            src, dst = own.at[ch, rows, :], emap.at[zz, me4, rows, :]
        else:
            src, dst = trunk.at[zz, ch, rows, :], emap.at[zz, me4, rows, pl.ds(off, W)]
        if k == 0:
            return pltpu.make_async_copy(src, dst, fr.at[j, zz, me4])
        return pltpu.make_async_remote_copy(
            src_ref=src, dst_ref=dst, send_sem=fs.at[j, zz, k], recv_sem=fr.at[j, zz, me4],
            device_id=(x, to), device_id_type=MESH)

    def fan_wait(j, zz, k, mine):
        if k == 0:
            fan_copy(j, zz, 0, mine).wait()
            return
        y2, c2 = peer(k)
        src4 = y2 * 2 + c2
        rows = rows_of(j)
        here = emap.at[zz, src4, rows, :] if mine else emap.at[zz, src4, rows, pl.ds(off, W)]
        pltpu.make_async_remote_copy(
            src_ref=here, dst_ref=here, send_sem=fs.at[j, zz, k], recv_sem=fr.at[j, zz, src4],
            device_id=(x, row), device_id_type=MESH).wait_recv()

    def x_copy(j, zz, at):
        here = emap.at[zz, :, rows_of(j), pl.ds(at, X)]
        return pltpu.make_async_remote_copy(
            src_ref=here, dst_ref=here, send_sem=xs.at[j, zz], recv_sem=xr.at[j, zz],
            device_id=(1 - x, row), device_id_type=MESH)

    def each_block(t, own_fn, other_fn):
        @pl.when(t == 0)
        def _():
            own_fn()

        @pl.when((t > 0) & (z - t >= 0))
        def _():
            other_fn(z - t, True)

        @pl.when((t > 0) & (z + t < Z))
        def _():
            other_fn(z + t, False)

    def can_go(up):
        return z < Z - 1 if up else z > 0

    def stage_a(j, t):
        def mine():
            for up in (True, False):
                @pl.when(can_go(up))
                def _():
                    z_copy(j, z, up, True).start()
            for k in (2, 3, 1, 0):
                fan_copy(j, z, k, True).start()

        def other(zz, up):
            z_wait(j, zz)

            @pl.when(can_go(up))
            def _():
                z_copy(j, zz, up, False).start()
            for k in (2, 3, 1, 0):
                fan_copy(j, zz, k, False).start()

        each_block(t, mine, other)

    def stage_b(j, t):
        def mine():
            for k in range(4):
                fan_wait(j, z, k, True)

        def other(zz, up):
            for k in range(4):
                fan_wait(j, zz, k, False)
            x_copy(j, zz, xoff).start()

        each_block(t, mine, other)

    low = lax.broadcasted_iota(jnp.int32, (KJ, 128), 1) < DEPTH

    def build(j, zz):
        jc = lax.div(j, J // JC)
        krows = pl.ds(pl.multiple_of(lax.rem(j, J // JC) * KJ, KJ), KJ)
        per = L // DEPTH

        def shard(s, _):
            for c in range(L // 128):
                a = emap[zz, s, rows_of(j), c * 128:(c + 1) * 128]
                b = pltpu.roll(a, DEPTH, 1)
                at = (zz * 4 + s) * per + 2 * c
                dup[jc, at, krows, :] = jnp.where(low, a, b)
                dup[jc, at + 1, krows, :] = jnp.where(low, b, a)
            return 0

        lax.fori_loop(0, 4, shard, 0)

    def stage_c(j, t):
        def mine():
            build(j, z)

        def other(zz, up):
            x_copy(j, zz, xland).wait_recv()
            build(j, zz)

        each_block(t, mine, other)

    N = J * Z

    def step(n):
        for lag, stage in ((0, stage_a), (1, stage_b), (2, stage_c)):
            m = n - lag

            @pl.when((m >= 0) & (m < N))
            def _(m=m, stage=stage):
                stage(lax.div(m, Z), lax.rem(m, Z))

    zero = dup.shape[1] - 1
    SL = 16
    lowc = lax.broadcasted_iota(jnp.int32, (KC, 128), 1) < DEPTH

    def multiply(jc, gp):
        def one(g):
            used = count[g]

            def some(q, acc):
                parts = []
                for p in range(SL // 2):
                    s = q * SL + 2 * p
                    i0 = jnp.where(s < used, light[g, s], zero)
                    i1 = jnp.where(s + 1 < used, light[g, s + 1], zero)
                    parts.append(jnp.where(lowc, dup[jc, i0], dup[jc, i1]))
                lhs = jnp.concatenate(parts, axis=1)
                rhs = tv[g, pl.ds(pl.multiple_of(q * SL * DEPTH, SL * DEPTH), SL * DEPTH), :]
                return acc + jnp.dot(lhs, rhs, preferred_element_type=jnp.float32)

            return lax.fori_loop(0, slots // SL, some, jnp.zeros((KC, 128), jnp.float32))

        a, b = one(2 * gp), one(2 * gp + 1)
        rows = pl.ds(pl.multiple_of(gp * 2 * fpd, 2 * fpd), 2 * fpd)
        for i in range(R // JC):
            both = jnp.concatenate([a[i * fpd:(i + 1) * fpd], b[i * fpd:(i + 1) * fpd]], axis=0)
            sb[jc * (R // JC) + i, rows, :] = both.astype(jnp.bfloat16)

    def out_copy(d):
        return pltpu.make_async_remote_copy(
            src_ref=sb.at[d], dst_ref=out.at[row], send_sem=os_.at[d], recv_sem=or_.at[row],
            device_id=(x, d), device_id_type=MESH)

    def out_local():
        return pltpu.make_async_copy(sb.at[row], out.at[row], or_.at[row])

    def send(jc):
        def one(i, _):
            d = jc * (R // JC) + lax.rem(row + i, R // JC)

            @pl.when(d != row)
            def _():
                out_copy(d).start()

            @pl.when(d == row)
            def _():
                out_local().start()
            return 0

        lax.fori_loop(0, R // JC, one, 0)

    GP = G // 2
    first = N // JC + 2
    rest = N + 2 - first
    per = max(1, rest // GP)

    for g in range(G):
        tile_copy(g).start()
    lax.fori_loop(0, first, lambda n, _: (step(n), 0)[1], 0)
    for g in range(G):
        tile_copy(g).wait()

    def second(i, _):
        step(first + i)

        @pl.when((lax.rem(i, per) == 0) & (lax.div(i, per) < GP))
        def _():
            multiply(0, lax.div(i, per))

        @pl.when(i == (GP - 1) * per)
        def _():
            send(0)
        return 0

    lax.fori_loop(0, rest, second, 0)
    lax.fori_loop(0, GP, lambda gp, _: (multiply(1, gp), 0)[1], 0)
    send(1)

    def drain(n, _):
        j, t = lax.div(n, Z), lax.rem(n, Z)

        def mine():
            for up in (True, False):
                @pl.when(can_go(up))
                def _():
                    z_copy(j, z, up, True).wait_send()
            for k in (1, 2, 3):
                fan_copy(j, z, k, True).wait_send()

        def other(zz, up):
            @pl.when(can_go(up))
            def _():
                z_copy(j, zz, up, False).wait_send()
            for k in (1, 2, 3):
                fan_copy(j, zz, k, False).wait_send()
            x_copy(j, zz, xoff).wait_send()

        each_block(t, mine, other)
        return 0

    lax.fori_loop(0, N, drain, 0)

    def finish(d, _):
        @pl.when(d != row)
        def _():
            out_copy(d).wait_send()
            pltpu.make_async_remote_copy(
                src_ref=out.at[d], dst_ref=out.at[d], send_sem=os_.at[d], recv_sem=or_.at[d],
                device_id=(x, d), device_id_type=MESH).wait_recv()

        @pl.when(d == row)
        def _():
            out_local().wait()
        return 0

    lax.fori_loop(0, R, finish, 0)


def fused(Z, W, tiles, tile_light, tile_count, env_maps, frame_slot):
    R = 4 * Z
    G, slots, depth, width = tiles.shape
    L = env_maps.shape[0]
    fpd = F // R
    bf = jnp.bfloat16
    dma = pltpu.SemaphoreType.DMA
    vmem = pl.BlockSpec(memory_space=pltpu.VMEM)
    smem = pl.BlockSpec(memory_space=pltpu.SMEM)
    pieces = pl.pallas_call(
        functools.partial(kernel, Z, W),
        out_shape=jax.ShapeDtypeStruct((R, G * fpd, width), bf),
        in_specs=[smem, smem, vmem, vmem, pl.BlockSpec(memory_space=pl.ANY)],
        out_specs=vmem,
        scratch_shapes=[
            pltpu.VMEM((CHANNELS, F, L), bf),
            pltpu.VMEM((Z, CHANNELS, F, W), bf),
            pltpu.VMEM((Z, 4, F, L), bf),
            pltpu.VMEM((JC, R * L // DEPTH + 1, F // JC, 128), bf),
            pltpu.VMEM((G, slots * depth, width), bf),
            pltpu.VMEM((R, G * fpd, width), bf),
            dma((J, 2, Z)), dma((J, Z)), dma((J, Z, 4)), dma((J, Z, 4)),
            dma((J, Z)), dma((J, Z)), dma((G,)), dma((R,)), dma((R,)),
        ],
        compiler_params=pltpu.CompilerParams(
            collective_id=0, has_side_effects=True, vmem_limit_bytes=56 * 1024 * 1024),
    )(tile_light, tile_count, frame_slot.reshape(F, 1), env_maps,
      tiles.reshape(G, slots * depth, width))
    return pieces.reshape(R, G, fpd, width).transpose(2, 0, 1, 3).reshape(fpd, R * G * width)


def plain(tiles, tile_light, tile_count, env_maps, frame_slot):
    blocks_dev, slots, depth, width = tiles.shape
    own_channel = lax.axis_index("row") % CHANNELS
    gathered = lax.all_gather(env_maps, "row", axis=0, tiled=True)
    whole = gathered.reshape(gathered.shape[0], CHANNELS, F)
    channel_map = lax.dynamic_index_in_dim(whole, own_channel, 1, keepdims=False)
    blocks = channel_map.reshape(channel_map.shape[0] // depth, depth, F)
    chosen = blocks[tile_light]
    active = (jnp.arange(slots, dtype=jnp.int32)[None, :] < tile_count[:, None]).astype(jnp.bfloat16)
    chosen = chosen * active[:, :, None, None]
    relit = jnp.einsum("gslr,gslf->fgr", tiles, chosen,
                       preferred_element_type=jnp.float32).astype(jnp.bfloat16)
    relit = relit[frame_slot].reshape(F, blocks_dev * width)
    return lax.all_to_all(relit, "row", split_axis=0, concat_axis=1, tiled=True)


def solution(mesh):
    rows, bands = mesh.shape["row"], mesh.shape["band"]

    def body(tiles, tile_light, tile_count, env_maps, frame_slot):
        L = env_maps.shape[0]
        fits = bands == 2 and rows % 8 == 0 and (F // rows) % 8 == 0 and L % 1024 == 0
        if not fits:
            return plain(tiles, tile_light, tile_count, env_maps, frame_slot)
        return fused(rows // 4, L * 5 // 8, tiles, tile_light, tile_count, env_maps, frame_slot)

    return jax.shard_map(
        body,
        mesh=mesh,
        in_specs=(
            P(("band", "row"), None, None, None),
            P(("band", "row"), None),
            P(("band", "row")),
            P("row", None),
            P(),
        ),
        out_specs=P("row", "band"),
        check_vma=False,
    )
```

```python
import functools
import jax
import jax.numpy as jnp
from jax import lax
from jax.experimental import pallas as pl
from jax.experimental.pallas import tpu as pltpu
from jax.sharding import PartitionSpec as P

F = 128
CHANNELS = 3
DEPTH = 64
J = 4
JC = 2
SUB = J // JC
LAG_B = 1
LAG_C = 3
MESH = pl.DeviceIdType.MESH


def kernel(Z, W, light, count, slot, env, tiles, out,
           own, trunk, emap, dup, tv, sb, zs, zr, fs, fr, xs, xr, ts, os_, or_):
    R = 4 * Z
    G, slots = light.shape
    L = env.shape[0]
    KJ = F // J
    KC = F // JC
    fpd = F // R
    X = L - W
    x = lax.axis_index("band")
    row = lax.axis_index("row")
    core = lax.rem(row, 2)
    y = lax.rem(lax.div(row, 2), 2)
    z = lax.div(row, 4)
    me4 = y * 2 + core
    mych = lax.rem(row, CHANNELS)
    off = pl.multiple_of(x * X, 128)
    xoff = pl.multiple_of(x * W, 128)
    xland = pl.multiple_of((1 - x) * W, 128)

    barrier = pltpu.get_barrier_semaphore()

    def greet(i, _):
        pl.semaphore_signal(barrier, inc=1, device_id=(x, lax.rem(row + i, R)), device_id_type=MESH)
        return 0

    lax.fori_loop(1, R, greet, 0)
    pl.semaphore_signal(barrier, inc=1, device_id=(1 - x, row), device_id_type=MESH)

    def tile_copy(g):
        return pltpu.make_async_copy(tiles.at[g], tv.at[g], ts.at[g])

    perm = (slot[...] == lax.broadcasted_iota(jnp.int32, (F, F), 1)).astype(jnp.float32).astype(jnp.bfloat16)
    for c in range(CHANNELS):
        own[c] = lax.dot_general(perm, env[:, c * F:(c + 1) * F], (((1,), (1,)), ((), ())),
                                 preferred_element_type=jnp.float32).astype(jnp.bfloat16)
    for jc in range(JC):
        dup[jc, dup.shape[1] - 1] = jnp.zeros((KC, 128), jnp.bfloat16)

    pl.semaphore_wait(barrier, R)

    def rows_of(j):
        return pl.ds(pl.multiple_of(j * KJ, KJ), KJ)

    def z_copy(j, zz, up, mine):
        rows = rows_of(j)
        src = own.at[:, rows, pl.ds(off, W)] if mine else trunk.at[zz, :, rows, :]
        to = row + 4 if up else row - 4
        return pltpu.make_async_remote_copy(
            src_ref=src, dst_ref=trunk.at[zz, :, rows, :],
            send_sem=zs.at[j, 0 if up else 1, zz], recv_sem=zr.at[j, zz],
            device_id=(x, to), device_id_type=MESH)

    def z_wait(j, zz):
        here = trunk.at[zz, :, rows_of(j), :]
        pltpu.make_async_remote_copy(
            src_ref=here, dst_ref=here, send_sem=zs.at[j, 0, zz], recv_sem=zr.at[j, zz],
            device_id=(x, row), device_id_type=MESH).wait_recv()

    def peer(k):
        y2 = 1 - y if k // 2 else y
        c2 = 1 - core if k % 2 else core
        return y2, c2

    def fan_copy(j, zz, k, mine):
        y2, c2 = peer(k)
        to = (z * 2 + y2) * 2 + c2
        ch = lax.rem(to, CHANNELS)
        rows = rows_of(j)
        if mine:
            src, dst = own.at[ch, rows, :], emap.at[zz, me4, rows, :]
        else:
            src, dst = trunk.at[zz, ch, rows, :], emap.at[zz, me4, rows, pl.ds(off, W)]
        if k == 0:
            return pltpu.make_async_copy(src, dst, fr.at[j, zz, me4])
        return pltpu.make_async_remote_copy(
            src_ref=src, dst_ref=dst, send_sem=fs.at[j, zz, k], recv_sem=fr.at[j, zz, me4],
            device_id=(x, to), device_id_type=MESH)

    def fan_wait(j, zz, k, mine):
        if k == 0:
            fan_copy(j, zz, 0, mine).wait()
            return
        y2, c2 = peer(k)
        src4 = y2 * 2 + c2
        rows = rows_of(j)
        here = emap.at[zz, src4, rows, :] if mine else emap.at[zz, src4, rows, pl.ds(off, W)]
        pltpu.make_async_remote_copy(
            src_ref=here, dst_ref=here, send_sem=fs.at[j, zz, k], recv_sem=fr.at[j, zz, src4],
            device_id=(x, row), device_id_type=MESH).wait_recv()

    def x_copy(j, zz, at):
        here = emap.at[zz, :, rows_of(j), pl.ds(at, X)]
        return pltpu.make_async_remote_copy(
            src_ref=here, dst_ref=here, send_sem=xs.at[j, zz], recv_sem=xr.at[j, zz],
            device_id=(1 - x, row), device_id_type=MESH)

    def each_block(t, own_fn, other_fn):
        @pl.when(t == 0)
        def _():
            own_fn()

        @pl.when((t > 0) & (z - t >= 0))
        def _():
            other_fn(z - t, True)

        @pl.when((t > 0) & (z + t < Z))
        def _():
            other_fn(z + t, False)

    def can_go(up):
        return z < Z - 1 if up else z > 0

    def own_out(j):
        for up in (True, False):
            @pl.when(can_go(up))
            def _():
                z_copy(j, z, up, True).start()

    def stage_a(j, t):
        def mine():
            for k in (2, 3, 1, 0):
                fan_copy(j, z, k, True).start()

        def other(zz, up):
            z_wait(j, zz)

            @pl.when(can_go(up))
            def _():
                z_copy(j, zz, up, False).start()
            for k in (2, 3, 1, 0):
                fan_copy(j, zz, k, False).start()

        each_block(t, mine, other)

        @pl.when((t == max(Z - 2, 0)) & (lax.rem(j, SUB) == SUB - 1) & (j < J - 1))
        def _():
            lax.fori_loop(0, SUB, lambda i, _: (own_out(j + 1 + i), 0)[1], 0)

    def stage_b(j, t):
        def mine():
            for k in range(4):
                fan_wait(j, z, k, True)

        def other(zz, up):
            for k in range(4):
                fan_wait(j, zz, k, False)
            x_copy(j, zz, xoff).start()

        each_block(t, mine, other)

    low = lax.broadcasted_iota(jnp.int32, (KJ, 128), 1) < DEPTH

    def build(j, zz):
        jc = lax.div(j, J // JC)
        krows = pl.ds(pl.multiple_of(lax.rem(j, J // JC) * KJ, KJ), KJ)
        per = L // DEPTH

        def shard(s, _):
            for c in range(L // 128):
                a = emap[zz, s, rows_of(j), c * 128:(c + 1) * 128]
                b = pltpu.roll(a, DEPTH, 1)
                at = (zz * 4 + s) * per + 2 * c
                dup[jc, at, krows, :] = jnp.where(low, a, b)
                dup[jc, at + 1, krows, :] = jnp.where(low, b, a)
            return 0

        lax.fori_loop(0, 4, shard, 0)

    def stage_c(j, t):
        def mine():
            build(j, z)

        def other(zz, up):
            x_copy(j, zz, xland).wait_recv()
            build(j, zz)

        each_block(t, mine, other)

    N = J * Z

    def step(n):
        for lag, stage in ((0, stage_a), (LAG_B, stage_b), (LAG_C, stage_c)):
            m = n - lag

            @pl.when((m >= 0) & (m < N))
            def _(m=m, stage=stage):
                stage(lax.div(m, SUB * Z) * SUB + lax.rem(m, SUB), lax.rem(lax.div(m, SUB), Z))

    zero = dup.shape[1] - 1
    SL = 32
    lowc = lax.broadcasted_iota(jnp.int32, (KC, 128), 1) < DEPTH

    def multiply(jc, gp):
        pair = (2 * gp, 2 * gp + 1)

        def some(q, accs):
            res = []
            for g, acc in zip(pair, accs):
                used = count[g]
                parts = []
                for p in range(SL // 2):
                    s = q * SL + 2 * p
                    i0 = jnp.where(s < used, light[g, s], zero)
                    i1 = jnp.where(s + 1 < used, light[g, s + 1], zero)
                    parts.append(jnp.where(lowc, dup[jc, i0], dup[jc, i1]))
                lhs = jnp.concatenate(parts, axis=1)
                rhs = tv[g, pl.ds(pl.multiple_of(q * SL * DEPTH, SL * DEPTH), SL * DEPTH), :]
                res.append(acc + jnp.dot(lhs, rhs, preferred_element_type=jnp.float32))
            return tuple(res)

        nil = jnp.zeros((KC, 128), jnp.float32)
        a, b = lax.fori_loop(0, slots // SL, some, (nil, nil))
        rows = pl.ds(pl.multiple_of(gp * 2 * fpd, 2 * fpd), 2 * fpd)
        for i in range(R // JC):
            both = jnp.concatenate([a[i * fpd:(i + 1) * fpd], b[i * fpd:(i + 1) * fpd]], axis=0)
            sb[jc * (R // JC) + i, rows, :] = both.astype(jnp.bfloat16)

    def out_copy(d):
        return pltpu.make_async_remote_copy(
            src_ref=sb.at[d], dst_ref=out.at[row], send_sem=os_.at[d], recv_sem=or_.at[row],
            device_id=(x, d), device_id_type=MESH)

    def out_local():
        return pltpu.make_async_copy(sb.at[row], out.at[row], or_.at[row])

    def send(jc):
        def one(i, _):
            d = jc * (R // JC) + lax.rem(row + i, R // JC)

            @pl.when(d != row)
            def _():
                out_copy(d).start()

            @pl.when(d == row)
            def _():
                out_local().start()
            return 0

        lax.fori_loop(0, R // JC, one, 0)

    GP = G // 2
    first = N // JC + LAG_C
    rest = N + LAG_C - first
    per = max(1, rest // GP)

    lax.fori_loop(0, SUB, lambda i, _: (own_out(i), 0)[1], 0)
    for g in range(G):
        tile_copy(g).start()
    lax.fori_loop(0, first, lambda n, _: (step(n), 0)[1], 0)
    for g in range(G):
        tile_copy(g).wait()

    def second(i, _):
        step(first + i)

        @pl.when((lax.rem(i, per) == 0) & (lax.div(i, per) < GP))
        def _():
            multiply(0, lax.div(i, per))

        @pl.when(i == (GP - 1) * per)
        def _():
            send(0)
        return 0

    lax.fori_loop(0, rest, second, 0)
    lax.fori_loop(0, GP, lambda gp, _: (multiply(1, gp), 0)[1], 0)
    send(1)

    def drain(n, _):
        j, t = lax.div(n, Z), lax.rem(n, Z)

        def mine():
            for up in (True, False):
                @pl.when(can_go(up))
                def _():
                    z_copy(j, z, up, True).wait_send()
            for k in (1, 2, 3):
                fan_copy(j, z, k, True).wait_send()

        def other(zz, up):
            @pl.when(can_go(up))
            def _():
                z_copy(j, zz, up, False).wait_send()
            for k in (1, 2, 3):
                fan_copy(j, zz, k, False).wait_send()
            x_copy(j, zz, xoff).wait_send()

        each_block(t, mine, other)
        return 0

    lax.fori_loop(0, N, drain, 0)

    def finish(d, _):
        @pl.when(d != row)
        def _():
            out_copy(d).wait_send()
            pltpu.make_async_remote_copy(
                src_ref=out.at[d], dst_ref=out.at[d], send_sem=os_.at[d], recv_sem=or_.at[d],
                device_id=(x, d), device_id_type=MESH).wait_recv()

        @pl.when(d == row)
        def _():
            out_local().wait()
        return 0

    lax.fori_loop(0, R, finish, 0)


def fused(Z, W, tiles, tile_light, tile_count, env_maps, frame_slot):
    R = 4 * Z
    G, slots, depth, width = tiles.shape
    L = env_maps.shape[0]
    fpd = F // R
    bf = jnp.bfloat16
    dma = pltpu.SemaphoreType.DMA
    vmem = pl.BlockSpec(memory_space=pltpu.VMEM)
    smem = pl.BlockSpec(memory_space=pltpu.SMEM)
    pieces = pl.pallas_call(
        functools.partial(kernel, Z, W),
        out_shape=jax.ShapeDtypeStruct((R, G * fpd, width), bf),
        in_specs=[smem, smem, vmem, vmem, pl.BlockSpec(memory_space=pl.ANY)],
        out_specs=vmem,
        scratch_shapes=[
            pltpu.VMEM((CHANNELS, F, L), bf),
            pltpu.VMEM((Z, CHANNELS, F, W), bf),
            pltpu.VMEM((Z, 4, F, L), bf),
            pltpu.VMEM((JC, R * L // DEPTH + 1, F // JC, 128), bf),
            pltpu.VMEM((G, slots * depth, width), bf),
            pltpu.VMEM((R, G * fpd, width), bf),
            dma((J, 2, Z)), dma((J, Z)), dma((J, Z, 4)), dma((J, Z, 4)),
            dma((J, Z)), dma((J, Z)), dma((G,)), dma((R,)), dma((R,)),
        ],
        compiler_params=pltpu.CompilerParams(
            collective_id=0, has_side_effects=True, vmem_limit_bytes=56 * 1024 * 1024),
    )(tile_light, tile_count, frame_slot.reshape(F, 1), env_maps,
      tiles.reshape(G, slots * depth, width))
    return pieces.reshape(R, G, fpd, width).transpose(2, 0, 1, 3).reshape(fpd, R * G * width)


def plain(tiles, tile_light, tile_count, env_maps, frame_slot):
    blocks_dev, slots, depth, width = tiles.shape
    own_channel = lax.axis_index("row") % CHANNELS
    gathered = lax.all_gather(env_maps, "row", axis=0, tiled=True)
    whole = gathered.reshape(gathered.shape[0], CHANNELS, F)
    channel_map = lax.dynamic_index_in_dim(whole, own_channel, 1, keepdims=False)
    blocks = channel_map.reshape(channel_map.shape[0] // depth, depth, F)
    chosen = blocks[tile_light]
    active = (jnp.arange(slots, dtype=jnp.int32)[None, :] < tile_count[:, None]).astype(jnp.bfloat16)
    chosen = chosen * active[:, :, None, None]
    relit = jnp.einsum("gslr,gslf->fgr", tiles, chosen,
                       preferred_element_type=jnp.float32).astype(jnp.bfloat16)
    relit = relit[frame_slot].reshape(F, blocks_dev * width)
    return lax.all_to_all(relit, "row", split_axis=0, concat_axis=1, tiled=True)


def solution(mesh):
    rows, bands = mesh.shape["row"], mesh.shape["band"]

    def body(tiles, tile_light, tile_count, env_maps, frame_slot):
        L = env_maps.shape[0]
        fits = bands == 2 and rows % 8 == 0 and (F // rows) % 8 == 0 and L % 1024 == 0
        if not fits:
            return plain(tiles, tile_light, tile_count, env_maps, frame_slot)
        return fused(rows // 4, L * 5 // 8, tiles, tile_light, tile_count, env_maps, frame_slot)

    return jax.shard_map(
        body,
        mesh=mesh,
        in_specs=(
            P(("band", "row"), None, None, None),
            P(("band", "row"), None),
            P(("band", "row")),
            P("row", None),
            P(),
        ),
        out_specs=P("row", "band"),
        check_vma=False,
    )
```

```python
import functools
import jax
import jax.numpy as jnp
from jax import lax
from jax.experimental import pallas as pl
from jax.experimental.pallas import tpu as pltpu
from jax.sharding import PartitionSpec as P

F = 128
CHANNELS = 3
DEPTH = 64
J = 4
JC = 2
SUB = J // JC
LAG_B = 3
LAG_C = 6
MESH = pl.DeviceIdType.MESH


def kernel(Z, W, light, count, slot, env_hbm, tiles, out,
           env, es, own, trunk, emap, dup, tv, sb, zs, zr, fs, fr, xs, xr, ts, os_, or_):
    R = 4 * Z
    G, slots = light.shape
    L = env_hbm.shape[0]
    KJ = F // J
    KC = F // JC
    fpd = F // R
    X = L - W
    x = lax.axis_index("band")
    row = lax.axis_index("row")
    core = lax.rem(row, 2)
    y = lax.rem(lax.div(row, 2), 2)
    z = lax.div(row, 4)
    me4 = y * 2 + core
    mych = lax.rem(row, CHANNELS)
    off = pl.multiple_of(x * X, 128)
    xoff = pl.multiple_of(x * W, 128)
    xland = pl.multiple_of((1 - x) * W, 128)

    load_env = pltpu.make_async_copy(env_hbm, env, es)
    load_env.start()
    barrier = pltpu.get_barrier_semaphore()

    def greet(i, _):
        pl.semaphore_signal(barrier, inc=1, device_id=(x, lax.rem(row + i, R)), device_id_type=MESH)
        return 0

    lax.fori_loop(1, R, greet, 0)
    pl.semaphore_signal(barrier, inc=1, device_id=(1 - x, row), device_id_type=MESH)

    def tile_copy(g):
        return pltpu.make_async_copy(tiles.at[g], tv.at[g], ts.at[g])

    perm = (slot[...] == lax.broadcasted_iota(jnp.int32, (F, F), 1)).astype(jnp.float32).astype(jnp.bfloat16)
    load_env.wait()
    for c in range(CHANNELS):
        own[c] = lax.dot_general(perm, env[:, c * F:(c + 1) * F], (((1,), (1,)), ((), ())),
                                 preferred_element_type=jnp.float32).astype(jnp.bfloat16)
    for jc in range(JC):
        dup[jc, dup.shape[1] - 1] = jnp.zeros((KC, 128), jnp.bfloat16)

    pl.semaphore_wait(barrier, R)

    def rows_of(j):
        return pl.ds(pl.multiple_of(j * KJ, KJ), KJ)

    def z_copy(j, zz, up, mine):
        rows = rows_of(j)
        src = own.at[:, rows, pl.ds(off, W)] if mine else trunk.at[zz, :, rows, :]
        to = row + 4 if up else row - 4
        return pltpu.make_async_remote_copy(
            src_ref=src, dst_ref=trunk.at[zz, :, rows, :],
            send_sem=zs.at[j, 0 if up else 1, zz], recv_sem=zr.at[j, zz],
            device_id=(x, to), device_id_type=MESH)

    def z_wait(j, zz):
        here = trunk.at[zz, :, rows_of(j), :]
        pltpu.make_async_remote_copy(
            src_ref=here, dst_ref=here, send_sem=zs.at[j, 0, zz], recv_sem=zr.at[j, zz],
            device_id=(x, row), device_id_type=MESH).wait_recv()

    def peer(k):
        y2 = 1 - y if k // 2 else y
        c2 = 1 - core if k % 2 else core
        return y2, c2

    def fan_copy(j, zz, k, mine):
        y2, c2 = peer(k)
        to = (z * 2 + y2) * 2 + c2
        ch = lax.rem(to, CHANNELS)
        rows = rows_of(j)
        if mine:
            src, dst = own.at[ch, rows, :], emap.at[zz, me4, rows, :]
        else:
            src, dst = trunk.at[zz, ch, rows, :], emap.at[zz, me4, rows, pl.ds(off, W)]
        if k == 0:
            return pltpu.make_async_copy(src, dst, fr.at[j, zz, me4])
        return pltpu.make_async_remote_copy(
            src_ref=src, dst_ref=dst, send_sem=fs.at[j, zz, k], recv_sem=fr.at[j, zz, me4],
            device_id=(x, to), device_id_type=MESH)

    def fan_wait(j, zz, k, mine):
        if k == 0:
            fan_copy(j, zz, 0, mine).wait()
            return
        y2, c2 = peer(k)
        src4 = y2 * 2 + c2
        rows = rows_of(j)
        here = emap.at[zz, src4, rows, :] if mine else emap.at[zz, src4, rows, pl.ds(off, W)]
        pltpu.make_async_remote_copy(
            src_ref=here, dst_ref=here, send_sem=fs.at[j, zz, k], recv_sem=fr.at[j, zz, src4],
            device_id=(x, row), device_id_type=MESH).wait_recv()

    def x_copy(j, zz, at):
        here = emap.at[zz, :, rows_of(j), pl.ds(at, X)]
        return pltpu.make_async_remote_copy(
            src_ref=here, dst_ref=here, send_sem=xs.at[j, zz], recv_sem=xr.at[j, zz],
            device_id=(1 - x, row), device_id_type=MESH)

    def each_block(t, own_fn, other_fn):
        @pl.when(t == 0)
        def _():
            own_fn()

        @pl.when((t > 0) & (z - t >= 0))
        def _():
            other_fn(z - t, True)

        @pl.when((t > 0) & (z + t < Z))
        def _():
            other_fn(z + t, False)

    def can_go(up):
        return z < Z - 1 if up else z > 0

    def own_out(j):
        for up in (True, False):
            @pl.when(can_go(up))
            def _():
                z_copy(j, z, up, True).start()

    def stage_a(j, t):
        def mine():
            for k in (0, 1, 2, 3):
                fan_copy(j, z, k, True).start()

        def other(zz, up):
            z_wait(j, zz)

            @pl.when(can_go(up))
            def _():
                z_copy(j, zz, up, False).start()
            for k in (0, 1, 2, 3):
                fan_copy(j, zz, k, False).start()

        each_block(t, mine, other)

        @pl.when((t == max(Z - 2, 0)) & (lax.rem(j, SUB) == SUB - 1) & (j < J - 1))
        def _():
            lax.fori_loop(0, SUB, lambda i, _: (own_out(j + 1 + i), 0)[1], 0)

    def stage_b(j, t):
        def mine():
            for k in range(4):
                fan_wait(j, z, k, True)

        def other(zz, up):
            for k in range(4):
                fan_wait(j, zz, k, False)
            x_copy(j, zz, xoff).start()

        each_block(t, mine, other)

    low = lax.broadcasted_iota(jnp.int32, (KJ, 128), 1) < DEPTH

    def build(j, zz):
        jc = lax.div(j, J // JC)
        krows = pl.ds(pl.multiple_of(lax.rem(j, J // JC) * KJ, KJ), KJ)
        per = L // DEPTH

        def shard(s, _):
            for c in range(L // 128):
                a = emap[zz, s, rows_of(j), c * 128:(c + 1) * 128]
                b = pltpu.roll(a, DEPTH, 1)
                at = (zz * 4 + s) * per + 2 * c
                dup[jc, at, krows, :] = jnp.where(low, a, b)
                dup[jc, at + 1, krows, :] = jnp.where(low, b, a)
            return 0

        lax.fori_loop(0, 4, shard, 0)

    def stage_c(j, t):
        def mine():
            build(j, z)

        def other(zz, up):
            x_copy(j, zz, xland).wait_recv()
            build(j, zz)

        each_block(t, mine, other)

    N = J * Z

    def step(n):
        for lag, stage in ((0, stage_a), (LAG_B, stage_b), (LAG_C, stage_c)):
            m = n - lag

            @pl.when((m >= 0) & (m < N))
            def _(m=m, stage=stage):
                stage(lax.div(m, SUB * Z) * SUB + lax.rem(m, SUB), lax.rem(lax.div(m, SUB), Z))

    zero = dup.shape[1] - 1
    SL = 32
    lowc = lax.broadcasted_iota(jnp.int32, (KC, 128), 1) < DEPTH

    def multiply(jc, gp):
        pair = (2 * gp, 2 * gp + 1)

        def some(q, accs):
            res = []
            for g, acc in zip(pair, accs):
                used = count[g]
                parts = []
                for p in range(SL // 2):
                    s = q * SL + 2 * p
                    i0 = jnp.where(s < used, light[g, s], zero)
                    i1 = jnp.where(s + 1 < used, light[g, s + 1], zero)
                    parts.append(jnp.where(lowc, dup[jc, i0], dup[jc, i1]))
                lhs = jnp.concatenate(parts, axis=1)
                rhs = tv[g, pl.ds(pl.multiple_of(q * SL * DEPTH, SL * DEPTH), SL * DEPTH), :]
                res.append(acc + jnp.dot(lhs, rhs, preferred_element_type=jnp.float32))
            return tuple(res)

        nil = jnp.zeros((KC, 128), jnp.float32)
        a, b = lax.fori_loop(0, slots // SL, some, (nil, nil))
        rows = pl.ds(pl.multiple_of(gp * 2 * fpd, 2 * fpd), 2 * fpd)
        for i in range(R // JC):
            both = jnp.concatenate([a[i * fpd:(i + 1) * fpd], b[i * fpd:(i + 1) * fpd]], axis=0)
            sb[jc * (R // JC) + i, rows, :] = both.astype(jnp.bfloat16)

    def rows_out(gp):
        return pl.ds(pl.multiple_of(gp * 2 * fpd, 2 * fpd), 2 * fpd)

    def out_copy(d, gp):
        rows = rows_out(gp)
        return pltpu.make_async_remote_copy(
            src_ref=sb.at[d, rows], dst_ref=out.at[row, rows], send_sem=os_.at[d, gp], recv_sem=or_.at[row, gp],
            device_id=(x, d), device_id_type=MESH)

    def out_local(gp):
        rows = rows_out(gp)
        return pltpu.make_async_copy(sb.at[row, rows], out.at[row, rows], or_.at[row, gp])

    def send(jc, gp):
        def one(i, _):
            d = jc * (R // JC) + lax.rem(row + i, R // JC)

            @pl.when(d != row)
            def _():
                out_copy(d, gp).start()

            @pl.when(d == row)
            def _():
                out_local(gp).start()
            return 0

        lax.fori_loop(0, R // JC, one, 0)

    GP = G // 2
    first = N // JC + LAG_C
    rest = N + LAG_C - max(first, G)
    per = max(1, rest // GP)

    lax.fori_loop(0, SUB, lambda i, _: (own_out(i), 0)[1], 0)

    def begin(n, _):
        step(n)

        @pl.when(n < G)
        def _():
            tile_copy(n).start()
        return 0

    lax.fori_loop(0, max(first, G), begin, 0)
    for g in range(G):
        tile_copy(g).wait()

    def second(i, _):
        step(max(first, G) + i)

        @pl.when((lax.rem(i, per) == 0) & (lax.div(i, per) < GP))
        def _():
            multiply(0, lax.div(i, per))
            send(0, lax.div(i, per))

        return 0

    lax.fori_loop(0, rest, second, 0)
    lax.fori_loop(0, GP, lambda gp, _: (multiply(1, gp), send(1, gp), 0)[2], 0)

    def drain(n, _):
        j, t = lax.div(n, Z), lax.rem(n, Z)

        def mine():
            for up in (True, False):
                @pl.when(can_go(up))
                def _():
                    z_copy(j, z, up, True).wait_send()
            for k in (1, 2, 3):
                fan_copy(j, z, k, True).wait_send()

        def other(zz, up):
            @pl.when(can_go(up))
            def _():
                z_copy(j, zz, up, False).wait_send()
            for k in (1, 2, 3):
                fan_copy(j, zz, k, False).wait_send()
            x_copy(j, zz, xoff).wait_send()

        each_block(t, mine, other)
        return 0

    lax.fori_loop(0, N, drain, 0)

    def finish(n, _):
        d, gp = lax.div(n, GP), lax.rem(n, GP)

        @pl.when(d != row)
        def _():
            out_copy(d, gp).wait_send()
            here = out.at[d, rows_out(gp)]
            pltpu.make_async_remote_copy(
                src_ref=here, dst_ref=here, send_sem=os_.at[d, gp], recv_sem=or_.at[d, gp],
                device_id=(x, d), device_id_type=MESH).wait_recv()

        @pl.when(d == row)
        def _():
            out_local(gp).wait()
        return 0

    lax.fori_loop(0, R * GP, finish, 0)


def fused(Z, W, tiles, tile_light, tile_count, env_maps, frame_slot):
    R = 4 * Z
    G, slots, depth, width = tiles.shape
    L = env_maps.shape[0]
    fpd = F // R
    bf = jnp.bfloat16
    dma = pltpu.SemaphoreType.DMA
    vmem = pl.BlockSpec(memory_space=pltpu.VMEM)
    hbm = pl.BlockSpec(memory_space=pl.ANY)
    smem = pl.BlockSpec(memory_space=pltpu.SMEM)
    pieces = pl.pallas_call(
        functools.partial(kernel, Z, W),
        out_shape=jax.ShapeDtypeStruct((R, G * fpd, width), bf),
        in_specs=[smem, smem, vmem, hbm, hbm],
        out_specs=vmem,
        scratch_shapes=[
            pltpu.VMEM(env_maps.shape, bf), dma(()),
            pltpu.VMEM((CHANNELS, F, L), bf),
            pltpu.VMEM((Z, CHANNELS, F, W), bf),
            pltpu.VMEM((Z, 4, F, L), bf),
            pltpu.VMEM((JC, R * L // DEPTH + 1, F // JC, 128), bf),
            pltpu.VMEM((G, slots * depth, width), bf),
            pltpu.VMEM((R, G * fpd, width), bf),
            dma((J, 2, Z)), dma((J, Z)), dma((J, Z, 4)), dma((J, Z, 4)),
            dma((J, Z)), dma((J, Z)), dma((G,)), dma((R, G // 2)), dma((R, G // 2)),
        ],
        compiler_params=pltpu.CompilerParams(
            collective_id=0, has_side_effects=True, vmem_limit_bytes=56 * 1024 * 1024),
    )(tile_light, tile_count, frame_slot.reshape(F, 1), env_maps,
      tiles.reshape(G, slots * depth, width))
    return pieces.reshape(R, G, fpd, width).transpose(2, 0, 1, 3).reshape(fpd, R * G * width)


def plain(tiles, tile_light, tile_count, env_maps, frame_slot):
    blocks_dev, slots, depth, width = tiles.shape
    own_channel = lax.axis_index("row") % CHANNELS
    gathered = lax.all_gather(env_maps, "row", axis=0, tiled=True)
    whole = gathered.reshape(gathered.shape[0], CHANNELS, F)
    channel_map = lax.dynamic_index_in_dim(whole, own_channel, 1, keepdims=False)
    blocks = channel_map.reshape(channel_map.shape[0] // depth, depth, F)
    chosen = blocks[tile_light]
    active = (jnp.arange(slots, dtype=jnp.int32)[None, :] < tile_count[:, None]).astype(jnp.bfloat16)
    chosen = chosen * active[:, :, None, None]
    relit = jnp.einsum("gslr,gslf->fgr", tiles, chosen,
                       preferred_element_type=jnp.float32).astype(jnp.bfloat16)
    relit = relit[frame_slot].reshape(F, blocks_dev * width)
    return lax.all_to_all(relit, "row", split_axis=0, concat_axis=1, tiled=True)


def solution(mesh):
    rows, bands = mesh.shape["row"], mesh.shape["band"]

    def body(tiles, tile_light, tile_count, env_maps, frame_slot):
        L = env_maps.shape[0]
        fits = bands == 2 and rows % 8 == 0 and (F // rows) % 8 == 0 and L % 1024 == 0
        if not fits:
            return plain(tiles, tile_light, tile_count, env_maps, frame_slot)
        return fused(rows // 4, L * 5 // 8, tiles, tile_light, tile_count, env_maps, frame_slot)

    return jax.shard_map(
        body,
        mesh=mesh,
        in_specs=(
            P(("band", "row"), None, None, None),
            P(("band", "row"), None),
            P(("band", "row")),
            P("row", None),
            P(),
        ),
        out_specs=P("row", "band"),
        check_vma=False,
    )
```
